32 devices in a mesh: ctx: 4 (over x, core), fsdp: 8 (over z, y).
Axes of the slice: x: 2, y: 2, z: 4, core: 2. Of those that a mesh axis runs over, the one named last changes fastest.
Arguments:
- tokens: bfloat16 [64, 512, 1024], P('fsdp', 'ctx'), may hold values from -8 to 8
- cotangent: bfloat16 [64, 512, 1024], P('fsdp', 'ctx'), may hold values from -8 to 8
- input_weight: bfloat16 [1024, 3072], P('fsdp'), may hold values from -0.25 to 0.25
- output_weight: bfloat16 [1024, 1024], P('fsdp'), may hold values from -1.5 to 1.5
- up_weight: bfloat16 [1024, 4096], P('fsdp'), may hold values from -0.1875 to 0.1875
- down_weight: bfloat16 [4096, 1024], P('fsdp'), may hold values from -0.125 to 0.125
- query_bias: bfloat16 [1024], P('fsdp'), may hold values from -3 to 3
- value_bias: bfloat16 [1024], P('fsdp'), may hold values from -3 to 3
- output_bias: bfloat16 [1024], P('fsdp'), may hold values from -3 to 3
- norm_gain: bfloat16 [1024], P('fsdp'), may hold values from 0.25 to 1.75
- norm_shift: bfloat16 [1024], P('fsdp'), may hold values from -1.75 to 1.75
- up_bias: bfloat16 [4096], P('fsdp'), may hold values from -3 to 3
- down_bias: bfloat16 [1024], P('fsdp'), may hold values from -1.75 to 1.75
- final_gain: bfloat16 [1024], P('fsdp'), may hold values from 0.25 to 1.75
- final_shift: bfloat16 [1024], P('fsdp'), may hold values from -1.75 to 1.75
Outputs:
- layer_out: bfloat16 [64, 512, 1024], P('fsdp', 'ctx')
- tokens_grad: bfloat16 [64, 512, 1024], P('fsdp', 'ctx')
- input_weight_grad: float32 [1024, 3072], P('fsdp')
- output_weight_grad: float32 [1024, 1024], P('fsdp')
- up_weight_grad: float32 [1024, 4096], P('fsdp')
- down_weight_grad: float32 [4096, 1024], P('fsdp')
- query_bias_grad: float32 [1024], P('fsdp')
- value_bias_grad: float32 [1024], P('fsdp')
- output_bias_grad: float32 [1024], P('fsdp')
- norm_gain_grad: float32 [1024], P('fsdp')
- norm_shift_grad: float32 [1024], P('fsdp')
- up_bias_grad: float32 [4096], P('fsdp')
- down_bias_grad: float32 [1024], P('fsdp')
- final_gain_grad: float32 [1024], P('fsdp')
- final_shift_grad: float32 [1024], P('fsdp')
The draws below stay inside these ranges and needn't reach their ends.
All inputs are finite; a program needn't handle non-finite values.
Results may differ from the reference program's by a relative error of at most 0.019.
The reference program's roundings to bfloat16 on the way count: a program that leaves them out, or rounds other values in their place, can miss the bound.
Values may be sent and summed in bfloat16 or wider, within the bound.
No kernel may reach another device: no remote copies, remote signals or barrier semaphores. Data moves between devices by JAX's collectives and lax.ppermute only.
A program may use at most 256 MiB of HBM per device.

```python
import math
import jax
import jax.numpy as jnp
from jax import lax

D = 1024
H = 16
HD = 64
FF = 4096
LEN = 512
SEQS = 64


def strengthened(drawn, own_key, source, target, blocks, factor):
    def block_of(axis_at):
        return (jnp.arange(drawn.shape[axis_at]) // (drawn.shape[axis_at] // blocks)).reshape((-1,) + (1,) * (drawn.ndim - 1 - axis_at))

    near = jax.random.permutation(own_key, blocks)[block_of(target)]
    other_side = (block_of(target) + blocks // 2) % blocks
    return jnp.where((block_of(source) == near) | (block_of(source) == other_side), factor * drawn, drawn)


def block_scale(own_key, extent, pieces, smallest, largest):
    level, own = 1.0, jax.random.fold_in(own_key, 6)
    for dim, shards_of in pieces:
        draws = jnp.exp(jax.random.uniform(jax.random.fold_in(own, dim), (shards_of,), jnp.float32, smallest / len(pieces), largest / len(pieces)))
        level = level * jnp.repeat(draws, extent[dim] // shards_of).reshape([-1 if axis == dim else 1 for axis in range(len(extent))])
    return level


def noise(key, shape, width, bound, split=(), held_as=jnp.bfloat16):
    values = jax.random.normal(key, shape, jnp.float32) * width
    if len(split) > 0:
        values = block_scale(key, shape, split, -0.22, 0.18) * values
    return jnp.clip(values, min=-bound, max=bound).astype(held_as)


def gaussian_with(own_key, dims, width, reach, cuts, heavy, kind=jnp.bfloat16):
    values = width * jax.random.normal(own_key, dims, jnp.float32)
    if cuts:
        values = values * block_scale(own_key, dims, cuts, -0.22, 0.18)
    return jnp.clip(strengthened(values, jax.random.fold_in(own_key, 3), *heavy), -reach, reach).astype(kind)


def setup_inputs(seed: int = 0) -> dict:
    splits = jax.random.split(jax.random.key(seed), 16)
    tokens = gaussian_with(splits[0], (SEQS, LEN, D), 1.0, 8.0, ((0, 8), (1, 4)), (0, 2, 8, 2.0))
    cotangent = gaussian_with(splits[1], (SEQS, LEN, D), 1.0, 8.0, ((0, 8), (1, 4)), (0, 2, 8, 2.0))
    input_weight = noise(splits[2], (D, 3 * D), (D // 2) ** -0.5, 0.25, ((0, 8),))
    output_weight = noise(splits[3], (D, D), (D // 64) ** -0.5, 1.5, ((0, 8),))
    up_weight = noise(splits[4], (D, FF), D ** -0.5, 0.1875, ((0, 8),))
    down_weight = noise(splits[5], (FF, D), (FF // 2) ** -0.5, 0.125, ((0, 8),))
    query_bias = noise(splits[6], (D,), 0.5, 3.0, ((0, 8),))
    value_bias = noise(splits[7], (D,), 0.5, 3.0, ((0, 8),))
    output_bias = noise(splits[8], (D,), 0.5, 3.0, ((0, 8),))
    norm_gain = jnp.clip(1.0 + 0.15 * jax.random.normal(splits[9], (D,), jnp.float32), 0.25, 1.75).astype(jnp.bfloat16)
    norm_shift = noise(splits[10], (D,), 0.3, 1.75, ((0, 8),))
    up_bias = noise(splits[11], (FF,), 0.5, 3.0, ((0, 8),))
    down_bias = noise(splits[12], (D,), 0.3, 1.75, ((0, 8),))
    final_gain = jnp.clip(1.0 + 0.15 * jax.random.normal(splits[13], (D,), jnp.float32), 0.25, 1.75).astype(jnp.bfloat16)
    final_shift = noise(splits[14], (D,), 0.3, 1.75, ((0, 8),))
    return dict(tokens=tokens, cotangent=cotangent, input_weight=input_weight, output_weight=output_weight, up_weight=up_weight, down_weight=down_weight, query_bias=query_bias, value_bias=value_bias, output_bias=output_bias, norm_gain=norm_gain, norm_shift=norm_shift, up_bias=up_bias, down_bias=down_bias, final_gain=final_gain, final_shift=final_shift)


@jax.custom_vjp
def low(v):
    return lax.optimization_barrier(v.astype(jnp.bfloat16)).astype(jnp.float32)

@jax.custom_vjp
def low_back(v):
    return v

def low_keep(v):
    return (low(v), None)

def low_pass(kept, grad):
    return (grad,)

def back_keep(v):
    return (v, None)

def back_low(kept, grad):
    return (low(grad),)
low.defvjp(low_keep, low_pass)
low_back.defvjp(back_keep, back_low)
epsilon = 1e-05

def matmul_high(left, right):
    return jnp.dot(left, right, precision=lax.Precision.HIGHEST, preferred_element_type=jnp.float32)

def layer_norm(values, gain, shift):
    centre = values - lax.optimization_barrier(jnp.mean(values, axis=-1, keepdims=True))
    spread = lax.optimization_barrier(jnp.mean(centre * centre, axis=-1, keepdims=True))
    return centre * lax.rsqrt(spread + epsilon) * gain + shift

def attend(triple):
    query, key_rows, value_rows = triple
    scores = jnp.einsum('qhd,khd->hqk', query, key_rows, precision=lax.Precision.HIGHEST, preferred_element_type=jnp.float32) * (1.0 / math.sqrt(HD))
    scores = low_back(scores)
    probs = jax.nn.softmax(scores, axis=-1)
    return jnp.einsum('hqk,khd->qhd', low(probs), value_rows, precision=lax.Precision.HIGHEST, preferred_element_type=jnp.float32)

def layer(tok_block, params):
    input_weight, output_weight, up_weight, down_weight, query_bias, value_bias, output_bias, norm_gain, norm_shift, up_bias, down_bias, final_gain, final_shift = params
    group = tok_block.shape[0]
    tok_rows = tok_block.reshape(group * LEN, D)
    merged = matmul_high(tok_rows, input_weight)
    query = low_back(low(merged[:, :D] + query_bias))
    key_rows = low_back(low(merged[:, D:2 * D]))
    value_rows = low_back(low(merged[:, 2 * D:] + value_bias))
    shaped = tuple((member.reshape(group, LEN, H, HD) for member in (query, key_rows, value_rows)))
    context = lax.map(jax.checkpoint(attend), shaped)
    context = low_back(low(context.reshape(group * LEN, D)))
    pre_one = tok_rows + low_back(matmul_high(context, output_weight)) + output_bias
    hidden = layer_norm(pre_one, norm_gain, norm_shift)
    inner = low_back(matmul_high(low(hidden), up_weight) + up_bias)
    active = low(jax.nn.gelu(inner, approximate=False))
    pre_two = hidden + low_back(matmul_high(active, down_weight)) + down_bias
    return layer_norm(pre_two, final_gain, final_shift).reshape(tok_block.shape)

def reference(tokens, cotangent, input_weight, output_weight, up_weight, down_weight, query_bias, value_bias, output_bias, norm_gain, norm_shift, up_bias, down_bias, final_gain, final_shift):
    params = tuple((weight.astype(jnp.float32) for weight in (input_weight, output_weight, up_weight, down_weight, query_bias, value_bias, output_bias, norm_gain, norm_shift, up_bias, down_bias, final_gain, final_shift)))
    group = math.gcd(SEQS, 8)
    blocks = tokens.astype(jnp.float32).reshape(SEQS // group, group, LEN, D)
    cot_blocks = cotangent.astype(jnp.float32).reshape(SEQS // group, group, LEN, D)

    def one_group(carry, pair):
        tok_block, cot_block = pair
        result, pull = jax.vjp(layer, tok_block, params)
        back_tokens, back_params = pull(cot_block)
        carry = tuple((held + fresh for held, fresh in zip(carry, back_params)))
        return (carry, (result.astype(jnp.bfloat16), back_tokens.astype(jnp.bfloat16)))
    start = tuple((jnp.zeros(weight.shape, jnp.float32) for weight in params))
    sums, (outputs, back_all) = lax.scan(one_group, start, (blocks, cot_blocks))
    return (outputs.reshape(SEQS, LEN, D), back_all.reshape(SEQS, LEN, D), sums[0], sums[1], sums[2], sums[3], sums[4], sums[5], sums[6], sums[7], sums[8], sums[9], sums[10], sums[11], sums[12])
```

```python
import math

import jax
import jax.numpy as jnp
from jax import lax
from jax.sharding import PartitionSpec as P

H = 16


epsilon = 1e-05


def norm_forward(values):
    centre = values - jnp.mean(values, axis=-1, keepdims=True)
    inverse = lax.rsqrt(jnp.mean(centre * centre, axis=-1, keepdims=True) + epsilon)
    return (centre * inverse, inverse)


def norm_backward(upstream, normed, inverse, gain):
    scaled = upstream * gain
    return inverse * (
        scaled
        - jnp.mean(scaled, axis=-1, keepdims=True)
        - normed * jnp.mean(scaled * normed, axis=-1, keepdims=True)
    )


def gelu_exact(values):
    return jax.nn.gelu(values, approximate=False)


def attend_forward(blocks):
    query, key_rows, value_rows = blocks
    factor = 1.0 / math.sqrt(query.shape[-1])
    scores = (
        jnp.einsum("sqhd,skhd->shqk", query, key_rows, preferred_element_type=jnp.float32) * factor
    )
    row_max = jnp.max(scores, axis=-1, keepdims=True)
    exponent = jnp.exp(scores - row_max)
    totals = jnp.sum(exponent, axis=-1, keepdims=True)
    probs = (exponent / totals).astype(jnp.bfloat16)
    context = jnp.einsum("shqk,skhd->sqhd", probs, value_rows, preferred_element_type=jnp.float32)
    return (context.astype(jnp.bfloat16), row_max + jnp.log(totals))


def attend_backward(blocks):
    query, key_rows, value_rows, d_context, log_total = blocks
    factor = 1.0 / math.sqrt(query.shape[-1])
    scores = (
        jnp.einsum("sqhd,skhd->shqk", query, key_rows, preferred_element_type=jnp.float32) * factor
    )
    probs = jnp.exp(scores - log_total)
    d_probs = jnp.einsum(
        "sqhd,skhd->shqk", d_context, value_rows, preferred_element_type=jnp.float32
    )
    centre = jnp.sum(probs * d_probs, axis=-1, keepdims=True)
    d_scores = (probs * (d_probs - centre)).astype(jnp.bfloat16)
    d_query = (
        jnp.einsum("shqk,skhd->sqhd", d_scores, key_rows, preferred_element_type=jnp.float32)
        * factor
    ).astype(jnp.bfloat16)
    d_keys = (
        jnp.einsum("shqk,sqhd->skhd", d_scores, query, preferred_element_type=jnp.float32) * factor
    ).astype(jnp.bfloat16)
    d_values = jnp.einsum(
        "shqk,sqhd->skhd", probs.astype(jnp.bfloat16), d_context, preferred_element_type=jnp.float32
    ).astype(jnp.bfloat16)
    return (d_query, d_keys, d_values)


def quarter(shard):
    rows = shard.shape[0] // lax.axis_size("ctx")
    return lax.dynamic_slice_in_dim(shard, lax.axis_index("ctx") * rows, rows, 0)


def gathered(shard):
    return lax.all_gather(quarter(shard), ("fsdp", "ctx"), axis=0, tiled=True)


def reduced(grad):
    part = lax.psum_scatter(
        grad.astype(jnp.bfloat16), ("fsdp", "ctx"), scatter_dimension=0, tiled=True
    )
    return lax.all_gather(part, "ctx", axis=0, tiled=True).astype(jnp.float32)


def local(
    tokens,
    cotangent,
    input_weight,
    output_weight,
    up_weight,
    down_weight,
    query_bias,
    value_bias,
    output_bias,
    norm_gain,
    norm_shift,
    up_bias,
    down_bias,
    final_gain,
    final_shift,
):
    small = (
        query_bias,
        value_bias,
        output_bias,
        norm_gain,
        norm_shift,
        up_bias,
        down_bias,
        final_gain,
        final_shift,
    )
    sizes = [member.shape[0] for member in small]
    ends = [sum(sizes[: i + 1]) for i in range(len(sizes))]
    all_small = lax.all_gather(jnp.concatenate(small), "fsdp", axis=0, tiled=False)
    (
        full_qbias,
        full_vbias,
        full_obias,
        full_ngain,
        full_nshift,
        full_ubias,
        full_dbias,
        full_fgain,
        full_fshift,
    ) = [
        all_small[:, end - size : end].reshape(-1).astype(jnp.float32)
        for size, end in zip(sizes, ends)
    ]
    mine = lax.all_to_all(tokens, "ctx", split_axis=0, concat_axis=1, tiled=True)
    mine_cot = lax.all_to_all(cotangent, "ctx", split_axis=0, concat_axis=1, tiled=True)
    wide_input = gathered(input_weight)
    wide_output = gathered(output_weight)
    wide_up = gathered(up_weight)
    wide_down = gathered(down_weight)
    seqs, length, width = mine.shape
    rows_all = seqs * length
    head_size = width // H
    tok_rows = mine.reshape(rows_all, width)
    merged = jnp.dot(tok_rows, wide_input, preferred_element_type=jnp.float32)
    query = (merged[:, :width] + full_qbias).astype(jnp.bfloat16)
    key_rows = merged[:, width : 2 * width].astype(jnp.bfloat16)
    value_rows = (merged[:, 2 * width :] + full_vbias).astype(jnp.bfloat16)
    shape = (seqs, 1, length, H, head_size)
    head_query = query.reshape(shape)
    head_keys = key_rows.reshape(shape)
    head_values = value_rows.reshape(shape)
    context, log_total = lax.map(attend_forward, (head_query, head_keys, head_values))
    context_rows = context.reshape(rows_all, width)
    pre_one = (
        tok_rows.astype(jnp.float32)
        + jnp.dot(context_rows, wide_output, preferred_element_type=jnp.float32)
        + full_obias
    )
    normed_one, inverse_one = norm_forward(pre_one)
    hidden = normed_one * full_ngain + full_nshift
    hidden_low = hidden.astype(jnp.bfloat16)
    inner = jnp.dot(hidden_low, wide_up, preferred_element_type=jnp.float32) + full_ubias
    active_full, gelu_pull = jax.vjp(gelu_exact, inner)
    active = active_full.astype(jnp.bfloat16)
    pre_two = hidden + jnp.dot(active, wide_down, preferred_element_type=jnp.float32) + full_dbias
    normed_two, inverse_two = norm_forward(pre_two)
    layer_out = (normed_two * full_fgain + full_fshift).astype(jnp.bfloat16).reshape(mine.shape)
    upstream = mine_cot.reshape(rows_all, width).astype(jnp.float32)
    final_gain_grad = jnp.sum(upstream * normed_two, axis=0)
    final_shift_grad = jnp.sum(upstream, axis=0)
    d_pre_two = norm_backward(upstream, normed_two, inverse_two, full_fgain)
    d_branch = d_pre_two.astype(jnp.bfloat16)
    down_bias_grad = jnp.sum(d_pre_two, axis=0)
    down_weight_grad = jnp.einsum("nf,nd->fd", active, d_branch, preferred_element_type=jnp.float32)
    d_active = jnp.einsum("nd,fd->nf", d_branch, wide_down, preferred_element_type=jnp.float32)
    d_inner = gelu_pull(d_active)[0].astype(jnp.bfloat16)
    up_bias_grad = jnp.sum(d_inner.astype(jnp.float32), axis=0)
    up_weight_grad = jnp.einsum(
        "nd,nf->df", hidden_low, d_inner, preferred_element_type=jnp.float32
    )
    d_hidden = d_pre_two + jnp.einsum(
        "nf,df->nd", d_inner, wide_up, preferred_element_type=jnp.float32
    )
    norm_gain_grad = jnp.sum(d_hidden * normed_one, axis=0)
    norm_shift_grad = jnp.sum(d_hidden, axis=0)
    d_pre_one = norm_backward(d_hidden, normed_one, inverse_one, full_ngain)
    d_attn = d_pre_one.astype(jnp.bfloat16)
    output_bias_grad = jnp.sum(d_pre_one, axis=0)
    output_weight_grad = jnp.einsum(
        "nc,nd->cd", context_rows, d_attn, preferred_element_type=jnp.float32
    )
    d_context = jnp.einsum(
        "nd,cd->nc", d_attn, wide_output, preferred_element_type=jnp.float32
    ).astype(jnp.bfloat16)
    head_dctx = d_context.reshape(shape)
    d_query, d_keys, d_values = lax.map(
        attend_backward, (head_query, head_keys, head_values, head_dctx, log_total)
    )
    d_query = d_query.reshape(rows_all, width)
    d_values = d_values.reshape(rows_all, width)
    d_merged = jnp.concatenate([d_query, d_keys.reshape(rows_all, width), d_values], axis=1)
    query_bias_grad = jnp.sum(d_query.astype(jnp.float32), axis=0)
    value_bias_grad = jnp.sum(d_values.astype(jnp.float32), axis=0)
    input_weight_grad = jnp.einsum(
        "nd,ne->de", tok_rows, d_merged, preferred_element_type=jnp.float32
    )
    tokens_grad = (
        d_pre_one
        + jnp.einsum("ne,de->nd", d_merged, wide_input, preferred_element_type=jnp.float32)
    ).astype(jnp.bfloat16)
    tokens_grad = tokens_grad.reshape(mine.shape)
    layer_out, tokens_grad = [
        lax.all_to_all(member, "ctx", split_axis=1, concat_axis=0, tiled=True)
        for member in (layer_out, tokens_grad)
    ]
    matrices = tuple(
        reduced(member)
        for member in (input_weight_grad, output_weight_grad, up_weight_grad, down_weight_grad)
    )
    vectors = (
        query_bias_grad,
        value_bias_grad,
        output_bias_grad,
        norm_gain_grad,
        norm_shift_grad,
        up_bias_grad,
        down_bias_grad,
        final_gain_grad,
        final_shift_grad,
    )
    parts = lax.axis_size("fsdp")
    joined = jnp.concatenate([member.reshape(parts, -1) for member in vectors], axis=1)
    summed = lax.psum(joined, ("fsdp", "ctx"))
    own = lax.dynamic_index_in_dim(summed, lax.axis_index("fsdp"), 0, keepdims=False)
    small_grads = tuple(own[end - size : end] for size, end in zip(sizes, ends))
    return (layer_out, tokens_grad) + matrices + small_grads


def solution(mesh):
    rows = P("fsdp", "ctx", None)
    matrix = P("fsdp", None)
    vector = P("fsdp")
    return jax.shard_map(
        local,
        mesh=mesh,
        in_specs=(rows,) * 2 + (matrix,) * 4 + (vector,) * 9,
        out_specs=(rows,) * 2 + (matrix,) * 4 + (vector,) * 9,
        check_vma=False,
    )
```

```python
import functools
import math

import jax
import jax.numpy as jnp
from jax import lax
from jax.experimental import pallas as pl
from jax.experimental.pallas import tpu as pltpu
from jax.sharding import PartitionSpec as P

HEAD = 64
EPSILON = 1e-05
LOW = jnp.bfloat16
WIDE = jnp.float32
NN = (((1,), (0,)), ((), ()))
NT = (((1,), (1,)), ((), ()))
TN = (((0,), (0,)), ((), ()))
PAD = 16


def dot(left, right, dims):
    return lax.dot_general(left, right, dims, preferred_element_type=WIDE)


def cost(flops, moved):
    scale = 16
    return pl.CostEstimate(
        flops=int(flops) // scale, bytes_accessed=int(moved) // scale, transcendentals=0
    )


def params(mib):
    return pltpu.CompilerParams(vmem_limit_bytes=mib << 20)


def struct(shape, dtype=LOW):
    return jax.ShapeDtypeStruct(tuple(shape), dtype)


def bits_of(size):
    return size.bit_length() - 1


ANYWHERE = pl.BlockSpec(memory_space=pl.ANY)


def placed(index, order):
    out = 0
    for bit in order:
        out = out * 2 + (index // 2**bit) % 2
    return out


def fetch(held_ref, parts, ranks, moves):
    for rank in range(ranks):

        def step(part, carry):
            for first, place, sem in moves:
                target = place(part, rank)
                source = held_ref.at[part * ranks + rank].at[:, pl.ds(first, target.shape[1])]
                pltpu.make_async_copy(source, target, sem).start()
            return carry

        lax.fori_loop(0, parts, step, 0)


def landed(target, sem):
    pltpu.make_async_copy(target, target, sem).wait()


def ds(index, size):
    return pl.ds(pl.multiple_of(index * size, size), size)


def fetch_input(held_ref, weight, sem, parts, ranks):
    width = weight.shape[0]
    rows, columns = width // parts, 3 * width // ranks

    def place(part, rank):
        return weight.at[ds(part, rows), pl.ds(rank * columns, columns)]

    fetch(held_ref, parts, ranks, [(0, place, sem)])
    landed(weight, sem)


def merge_kernel(tok_ref, bias_ref, held_ref, *refs, parts, ranks):
    q_ref, k_ref, v_ref, weight, sem = refs[-5:]
    width = tok_ref.shape[1]

    @pl.when(pl.program_id(0) == 0)
    def _():
        fetch_input(held_ref, weight, sem, parts, ranks)

    rows = tok_ref[...]
    for at, out in enumerate((q_ref, k_ref, v_ref)):
        value = dot(rows, weight[:, at * width : (at + 1) * width], NN)
        if at != 1:
            value = value + bias_ref[at : at + 1, :].astype(WIDE)
        out[...] = value.astype(LOW)


def merge(tok, held, bias, parts, ranks, after, tile=256):
    rows, width = tok.shape
    row = pl.BlockSpec((tile, width), lambda i: (i, 0))
    return pl.pallas_call(
        functools.partial(merge_kernel, parts=parts, ranks=ranks),
        grid=(rows // tile,),
        in_specs=[row, pl.BlockSpec(bias.shape, lambda i: (0, 0))]
        + [ANYWHERE] * (1 + len(after)),
        out_specs=[row] * 3,
        out_shape=[struct(tok.shape)] * 3,
        scratch_shapes=[pltpu.VMEM((width, 3 * width), LOW), pltpu.SemaphoreType.DMA],
        compiler_params=params(60),
        cost_estimate=cost(6 * rows * width * width, 14 * rows * width),
        name="merge",
    )(tok, bias, held, *after)


def attend_forward_kernel(q_ref, k_ref, v_ref, o_ref):
    shape = o_ref.shape
    query, keys, values = [ref[...].reshape(-1, 2 * HEAD) for ref in (q_ref, k_ref, v_ref)]
    first = lax.broadcasted_iota(jnp.int32, query.shape, 1) < HEAD
    zero = jnp.zeros_like(query)
    outs = []
    for one in (jnp.where(first, query, zero), jnp.where(first, zero, query)):
        scores = dot(one, keys, NT)
        peak = jnp.max(scores, axis=1, keepdims=True)
        raised = jnp.exp((scores - peak) * (1.0 / math.sqrt(HEAD)))
        total = jnp.sum(raised, axis=1, keepdims=True)
        outs.append(dot(raised.astype(LOW), values, NN) * (1.0 / total))
    o_ref[...] = jnp.where(first, outs[0], outs[1]).astype(LOW).reshape(shape)


def head_spec(shape):
    pieces, _, length, _ = shape
    return pl.BlockSpec((pieces, 1, length, 2 * HEAD), lambda s, h: (0, s, 0, h))


def attend_forward(query, keys, values, shape):
    spec = head_spec(shape)
    rows = math.prod(shape[:3])
    area = rows * shape[0] * shape[2] * shape[3]
    return pl.pallas_call(
        attend_forward_kernel,
        grid=(shape[1], shape[3] // (2 * HEAD)),
        in_specs=[spec] * 3,
        out_specs=spec,
        out_shape=struct(shape),
        compiler_params=params(60),
        cost_estimate=cost(16 * area, 8 * rows * shape[3]),
        name="attend_forward",
    )(*[member.reshape(shape) for member in (query, keys, values)])


def attend_backward_kernel(q_ref, k_ref, v_ref, c_ref, *refs):
    dq_ref, dk_ref, dv_ref, qs_ref, vs_ref, mark_ref = refs[-6:]
    mark_ref[...] = jnp.zeros_like(mark_ref)
    shape = dq_ref.shape
    query, keys, values, d_context = [
        ref[...].reshape(-1, 2 * HEAD) for ref in (q_ref, k_ref, v_ref, c_ref)
    ]
    first = lax.broadcasted_iota(jnp.int32, query.shape, 1) < HEAD
    zero = jnp.zeros_like(query)
    factor = 1.0 / math.sqrt(HEAD)
    outs = []
    for head in range(2):

        def only(value):
            return jnp.where(first, value, zero) if head == 0 else jnp.where(first, zero, value)

        scores = dot(keys, only(query), NT)
        peak = jnp.max(scores, axis=0, keepdims=True)
        raised = jnp.exp((scores - peak) * factor)
        probs = raised * (1.0 / jnp.sum(raised, axis=0, keepdims=True))
        d_probs = dot(values, only(d_context), NT)
        product = probs * d_probs
        d_scores = (product - probs * jnp.sum(product, axis=0, keepdims=True)).astype(LOW)
        outs.append(
            (
                dot(d_scores, keys, TN),
                dot(d_scores, query, NN),
                dot(probs.astype(LOW), d_context, NN),
            )
        )
    d_query = (jnp.where(first, outs[0][0], outs[1][0]) * factor).astype(LOW)
    d_keys = (jnp.where(first, outs[0][1], outs[1][1]) * factor).astype(LOW)
    d_values = jnp.where(first, outs[0][2], outs[1][2]).astype(LOW)
    dq_ref[...] = d_query.reshape(shape)
    dk_ref[...] = d_keys.reshape(shape)
    dv_ref[...] = d_values.reshape(shape)
    for value, out in ((d_query, qs_ref), (d_values, vs_ref)):
        total = jnp.sum(value.astype(WIDE), axis=0, keepdims=True)
        out[...] = jnp.broadcast_to(total, (8, 2 * HEAD))


def attend_backward(query, keys, values, d_context, shape, share, begun, after):
    pieces, count, length, width = shape
    pairs = width // (2 * HEAD) // 2
    sequence, first = share // 2, share % 2 * pairs
    spec = pl.BlockSpec((pieces, 1, length, 2 * HEAD), lambda h: (0, sequence, 0, first + h))
    sums = pl.BlockSpec((8, 2 * HEAD), lambda h: (sequence, first + h))
    rows = math.prod(shape[:3])
    area = rows * pieces * length * width // count // 2
    return pl.pallas_call(
        attend_backward_kernel,
        grid=(pairs,),
        in_specs=[spec] * 4 + [ANYWHERE] * (len(begun) + len(after)),
        out_specs=[spec] * 3 + [sums] * 2 + [pl.BlockSpec((8, 2 * HEAD), lambda h: (0, 0))],
        out_shape=[struct(shape)] * 3
        + [struct((8 * count, width), WIDE)] * 2
        + [struct((8, 2 * HEAD), WIDE)],
        input_output_aliases={4 + at: at for at in range(len(begun))},
        compiler_params=params(60),
        cost_estimate=cost(40 * area, 14 * rows * width // count),
        name="attend_backward",
    )(*[member.reshape(shape) for member in (query, keys, values, d_context)], *begun, *after)


def gelu_and_slope(value):
    raised = jnp.exp(value * value * -0.5)
    at = 1.0 / (1.0 + (0.3275911 * math.sqrt(0.5)) * jnp.abs(value))
    series = 0.5 * -1.453152027 + at * (0.5 * 1.061405429)
    for term in (1.421413741, -0.284496736, 0.254829592):
        series = 0.5 * term + at * series
    tail = at * series * raised
    below = jnp.where(value >= 0, 1.0 - tail, tail)
    return value * below, below + value * raised * (1.0 / math.sqrt(2.0 * math.pi))


def mean(value):
    return jnp.mean(value, axis=1, keepdims=True)


def total(value):
    return jnp.sum(value, axis=0, keepdims=True)


def norm_forward(value):
    centre = value - mean(value)
    inverse = lax.rsqrt(mean(centre * centre) + EPSILON)
    return centre * inverse, inverse


def norm_backward(upstream, normed, inverse, gain):
    scaled = upstream * gain
    return inverse * (scaled - mean(scaled) - normed * mean(scaled * normed))


def middle_kernel(
    context_ref,
    tok_ref,
    cot_ref,
    vector_ref,
    up_bias_ref,
    *refs,
    parts,
    ranks,
    chunk,
):
    held_ref, refs = refs[0], refs[-15:]
    (
    out_ref,
    hidden_ref,
    active_ref,
    d_branch_ref,
    d_inner_ref,
    d_attn_ref,
    d_context_ref,
    d_pre_ref,
    sums_ref,
    up_sums_ref,
    output_weight,
    up_weight,
    down_weight,
    slope_ref,
    sems,
    ) = refs
    width, inner_width = up_weight.shape
    start = pl.program_id(0) == 0

    @pl.when(start)
    def _():
        own = width // parts
        span, narrow = inner_width // ranks, width // ranks
        fetch(
            held_ref,
            parts,
            ranks,
            [
                (
                    span,
                    lambda part, rank: output_weight.at[
                        ds(part, own), pl.ds(rank * narrow, narrow)
                    ],
                    sems.at[0],
                ),
                (
                    0,
                    lambda part, rank: up_weight.at[ds(part, own), pl.ds(rank * span, span)],
                    sems.at[1],
                ),
                (
                    span + narrow,
                    lambda part, rank: down_weight.at[ds(part * ranks + rank, own), :],
                    sems.at[2],
                ),
            ],
        )
        sums_ref[...] = jnp.zeros_like(sums_ref)
        up_sums_ref[...] = jnp.zeros_like(up_sums_ref)
        landed(output_weight, sems.at[0])

    output_bias, norm_gain, norm_shift, down_bias, final_gain, final_shift = [
        vector_ref[at : at + 1, :].astype(WIDE) for at in range(2, 8)
    ]
    pre_one = (
        tok_ref[...].astype(WIDE) + dot(context_ref[...], output_weight[...], NN) + output_bias
    )
    normed_one, inverse_one = norm_forward(pre_one)
    hidden = normed_one * norm_gain + norm_shift
    hidden_low = hidden.astype(LOW)
    hidden_ref[...] = hidden_low

    @pl.when(start)
    def _():
        landed(up_weight, sems.at[1])
        landed(down_weight, sems.at[2])

    branch = hidden + down_bias
    for at in range(0, inner_width, chunk):
        span = slice(at, at + chunk)
        inner = dot(hidden_low, up_weight[:, span], NN) + up_bias_ref[:, span].astype(WIDE)
        active, slope = gelu_and_slope(inner)
        active = active.astype(LOW)
        active_ref[:, span] = active
        slope_ref[:, span] = slope
        branch = branch + dot(active, down_weight[span, :], NN)
    normed_two, inverse_two = norm_forward(branch)
    out_ref[...] = (normed_two * final_gain + final_shift).astype(LOW)
    upstream = cot_ref[...].astype(WIDE)
    d_pre_two = norm_backward(upstream, normed_two, inverse_two, final_gain)
    d_branch = d_pre_two.astype(LOW)
    d_branch_ref[...] = d_branch
    d_hidden = d_pre_two
    for at in range(0, inner_width, chunk):
        span = slice(at, at + chunk)
        d_inner = (dot(d_branch, down_weight[span, :], NT) * slope_ref[:, span]).astype(LOW)
        d_inner_ref[:, span] = d_inner
        up_sums_ref[:, span] += total(d_inner.astype(WIDE))
        d_hidden = d_hidden + dot(d_inner, up_weight[:, span], NT)
    d_pre_one = norm_backward(d_hidden, normed_one, inverse_one, norm_gain)
    d_attn = d_pre_one.astype(LOW)
    d_attn_ref[...] = d_attn
    d_pre_ref[...] = d_pre_one
    d_context_ref[...] = dot(d_attn, output_weight[...], NT).astype(LOW)
    sums = (
        d_pre_one,
        d_hidden * normed_one,
        d_hidden,
        d_pre_two,
        upstream * normed_two,
        upstream,
    )
    for at, value in enumerate(sums):
        sums_ref[at : at + 1, :] += total(value)


def middle(context, tok, cot, held, vectors, up_bias, parts, ranks, tile=256):
    rows, width = tok.shape
    inner_width = up_bias.shape[1]
    row = pl.BlockSpec((tile, width), lambda i: (i, 0))
    broad = pl.BlockSpec((tile, inner_width), lambda i: (i, 0))

    def whole(shape):
        return pl.BlockSpec(shape, lambda i: (0, 0))

    low, deep = struct((rows, width)), struct((rows, inner_width))
    return pl.pallas_call(
        functools.partial(middle_kernel, parts=parts, ranks=ranks, chunk=1024),
        grid=(rows // tile,),
        in_specs=[row] * 3 + [whole(vectors.shape), whole(up_bias.shape), ANYWHERE],
        out_specs=[row, row, broad, row, broad, row, row, row]
        + [whole((8, width)), whole((1, inner_width))],
        scratch_shapes=[
            pltpu.VMEM((width, width), LOW),
            pltpu.VMEM((width, inner_width), LOW),
            pltpu.VMEM((inner_width, width), LOW),
            pltpu.VMEM((tile, inner_width), WIDE),
            pltpu.SemaphoreType.DMA((3,)),
        ],
        out_shape=[low, low, deep, low, deep, low, low, struct((rows, width), WIDE)]
        + [struct((8, width), WIDE), struct((1, inner_width), WIDE)],
        compiler_params=params(60),
        cost_estimate=cost(
            4 * rows * width * (2 * inner_width + width), 18 * width * inner_width * rows // 1024
        ),
        name="middle",
    )(context, tok, cot, vectors, up_bias, held)


def down_grad_kernel(half_ref, near_ref, far_ref, active_ref, *refs):
    out_near, out_far, turned = refs[-3:]
    columns = near_ref.shape[1]

    @pl.when(pl.program_id(0) == 0)
    def _():
        turned[:columns] = near_ref[...].T
        turned[columns:] = far_ref[...].T

    group, _, _, deep = out_near.shape
    result = dot(turned[...], active_ref[...], NN).astype(LOW)
    for part in range(group):
        at = placed(part, range(bits_of(group)))
        span = slice(part * deep, (part + 1) * deep)
        out_near[at, 0] = result[:columns, span]
        out_far[at, 0] = result[columns:, span]


def down_grad(half, active, d_branch, parts, order, after):
    rows, inner_width = active.shape
    columns = d_branch.shape[1] // 2
    deep = inner_width // parts
    group = max(1, 1024 // deep)
    steps = parts // group
    low = bits_of(group)
    order = tuple(range(low)) + tuple(bit for bit in order if bit >= low)
    high = [bit - low for bit in order[low:]]
    out = pl.BlockSpec((group, 1, columns, deep), lambda i, half: (0, placed(i, high), 0, 0))
    near, far = pl.pallas_call(
        down_grad_kernel,
        grid_spec=pltpu.PrefetchScalarGridSpec(
            num_scalar_prefetch=1,
            grid=(steps,),
            in_specs=[
                pl.BlockSpec((rows, columns), lambda i, half: (0, half[0])),
                pl.BlockSpec((rows, columns), lambda i, half: (0, 1 - half[0])),
                pl.BlockSpec((rows, group * deep), lambda i, half: (0, i)),
            ]
            + [ANYWHERE] * len(after),
            out_specs=[out, out],
            scratch_shapes=[pltpu.VMEM((2 * columns, rows), LOW)],
        ),
        out_shape=[struct((group, steps, columns, deep))] * 2,
        compiler_params=params(60),
        cost_estimate=cost(4 * rows * inner_width * columns, 4 * rows * inner_width),
        name="down_grad",
    )(half, d_branch, d_branch, active, *after)
    return near.reshape(parts, columns, deep), far.reshape(parts, columns, deep), order


def spread(result, out_ref, order):
    rows = result.shape[0] // 2 ** len(order)
    for part in range(2 ** len(order)):
        out_ref[placed(part, order)] = result[part * rows : (part + 1) * rows]


def output_grad_kernel(half_ref, context_ref, *refs, order, chips):
    grads, (far_ref, near_ref, turned) = refs[:2], refs[-3:]
    at = pl.program_id(0)

    @pl.when(at == 0)
    def _():
        turned[...] = context_ref[...].T
        spread(dot(turned[...], grads[0][...], NN).astype(LOW), far_ref.at[0], order)

    for chip in range(chips):
        for side, out_ref in ((0, far_ref), (1, near_ref)):
            if chip + side > 0:

                @pl.when(at == side * chips + chip)
                def _():
                    spread(dot(turned[...], grads[side][...], NN).astype(LOW), out_ref.at[0], order)


def output_grad(half, context, d_attn, near, far, parts, ranks, order, after):
    rows, width = context.shape
    chips, narrow, own = ranks // 2, width // ranks, width // parts
    shape = (chips, parts, own, near.shape[2])
    last = shape[3] // narrow - 1
    block = (1, parts, own, narrow)

    def far_at(i):
        return jnp.minimum(i, chips - 1)

    def near_at(i):
        return jnp.maximum(i - chips, 0)

    far, near = pl.pallas_call(
        functools.partial(output_grad_kernel, order=order, chips=chips),
        grid_spec=pltpu.PrefetchScalarGridSpec(
            num_scalar_prefetch=1,
            grid=(ranks,),
            in_specs=[
                pl.BlockSpec((rows, width), lambda i, half: (0, 0)),
                pl.BlockSpec((rows, narrow), lambda i, half: (0, 2 * far_at(i) + 1 - half[0])),
                pl.BlockSpec((rows, narrow), lambda i, half: (0, 2 * near_at(i) + half[0])),
            ]
            + [ANYWHERE] * (2 + len(after)),
            out_specs=[
                pl.BlockSpec(block, lambda i, half: (far_at(i), 0, 0, last)),
                pl.BlockSpec(block, lambda i, half: (near_at(i), 0, 0, last)),
            ],
            scratch_shapes=[pltpu.VMEM((width, rows), LOW)],
        ),
        out_shape=[struct(shape)] * 2,
        input_output_aliases={4: 0, 5: 1},
        compiler_params=params(40),
        cost_estimate=cost(2 * rows * width * width, 6 * rows * width),
        name="output_grad",
    )(half, context, d_attn, d_attn, far.reshape(shape), near.reshape(shape), *after)
    return [member.reshape(-1, own, shape[3]) for member in (near, far)]


def up_grad_kernel(half_ref, hidden_ref, grad_ref, *refs, order, chips):
    far_ref, near_ref, turned = refs[-3:]
    at = pl.program_id(0)

    @pl.when(at == 0)
    def _():
        turned[...] = hidden_ref[...].T

    for first, out_ref in ((0, far_ref), (chips, near_ref)):

        @pl.when((at >= first) & (at < first + chips))
        def _():
            spread(dot(turned[...], grad_ref[...], NN).astype(LOW), out_ref.at[0], order)


def up_grad(half, hidden_low, d_inner, parts, ranks, order, extra, after):
    rows, width = hidden_low.shape
    columns = d_inner.shape[1] // ranks
    chips = ranks // 2

    def column(i, half):
        far = i < chips
        return 0, jnp.where(far, 2 * i + 1 - half[0], 2 * (i - chips) + half[0])

    block = (1, parts, width // parts, columns)
    far, near = pl.pallas_call(
        functools.partial(up_grad_kernel, order=order, chips=chips),
        grid_spec=pltpu.PrefetchScalarGridSpec(
            num_scalar_prefetch=1,
            grid=(ranks,),
            in_specs=[
                pl.BlockSpec((rows, width), lambda i, half: (0, 0)),
                pl.BlockSpec((rows, columns), column),
            ]
            + [ANYWHERE] * len(after),
            out_specs=[
                pl.BlockSpec(block, lambda i, half: (jnp.minimum(i, chips - 1), 0, 0, 0)),
                pl.BlockSpec(block, lambda i, half: (jnp.maximum(i - chips, 0), 0, 0, 0)),
            ],
            scratch_shapes=[pltpu.VMEM((width, rows), LOW)],
        ),
        out_shape=[struct((chips,) + block[1:3] + (columns + extra,))] * 2,
        compiler_params=params(60),
        cost_estimate=cost(2 * rows * width * columns * ranks, 4 * rows * columns * ranks),
        name="up_grad",
    )(half, hidden_low, d_inner, *after)
    return [member.reshape(-1, width // parts, columns + extra) for member in (near, far)]


def input_grad_kernel(half_ref, tok_ref, *refs, order, chips):
    grads, outs, turned = refs[:6], refs[-5:-1], refs[-1]
    at = pl.program_id(0)

    @pl.when(at == 0)
    def _():
        turned[...] = tok_ref[...].T

    for side in range(2):
        for step in range(2 + chips):

            @pl.when(at == side * (2 + chips) + step)
            def _():
                grad_ref = grads[3 * side + min(step, 2)]
                out_ref = outs[2 * side] if step < 2 else outs[2 * side + 1].at[0]
                spread(dot(turned[...], grad_ref[...], NN).astype(LOW), out_ref, order)


def input_grad(half, tok, d_query, d_values, d_keys, parts, ranks, order, after):
    rows, width = tok.shape
    columns, narrow = width // 2, width // ranks
    own = width // parts
    chips = ranks // 2
    steps = 2 + chips

    def key_at(i, side):
        return jnp.clip(i - side * steps - 2, 0, chips - 1)

    ins, out_specs, outs = [], [], []
    for side in range(2):

        def core(half, side=side):
            return half[0] if side else 1 - half[0]

        ins += [pl.BlockSpec((rows, columns), lambda i, half, core=core: (0, core(half)))] * 2
        ins += [
            pl.BlockSpec(
                (rows, narrow),
                lambda i, half, core=core, side=side: (0, 2 * key_at(i, side) + core(half)),
            )
        ]
        out_specs += [
            pl.BlockSpec(
                (parts, own, columns),
                lambda i, half, side=side: (0, jnp.clip(i - side * steps, 0, 1), 0),
            ),
            pl.BlockSpec(
                (1, parts, own, narrow), lambda i, half, side=side: (key_at(i, side), 0, 0, 0)
            ),
        ]
        outs += [struct((parts, 2 * own + PAD, columns)), struct((chips, parts, own, narrow))]
    far, far_keys, near, near_keys = pl.pallas_call(
        functools.partial(input_grad_kernel, order=order, chips=chips),
        grid_spec=pltpu.PrefetchScalarGridSpec(
            num_scalar_prefetch=1,
            grid=(2 * steps,),
            in_specs=[pl.BlockSpec((rows, width), lambda i, half: (0, 0))]
            + ins
            + [ANYWHERE] * len(after),
            out_specs=out_specs,
            scratch_shapes=[pltpu.VMEM((width, rows), LOW)],
        ),
        out_shape=outs,
        compiler_params=params(40),
        cost_estimate=cost(6 * rows * width * width, 10 * rows * width),
        name="input_grad",
    )(half, tok, *[d_query, d_values, d_keys] * 2, *after)
    shape = (-1, own, narrow)
    return near, far, near_keys.reshape(shape), far_keys.reshape(shape)


def tokens_grad_kernel(d_pre_ref, dq_ref, dk_ref, dv_ref, held_ref, *refs, parts, ranks):
    out_ref, weight, sem = refs[-3:]
    width = d_pre_ref.shape[1]

    @pl.when(pl.program_id(0) == 0)
    def _():
        fetch_input(held_ref, weight, sem, parts, ranks)

    value = d_pre_ref[...]
    for at, ref in enumerate((dq_ref, dk_ref, dv_ref)):
        value = value + dot(ref[...], weight[:, at * width : (at + 1) * width], NT)
    out_ref[...] = value.astype(LOW)


def tokens_grad_of(d_pre_one, grads, held, parts, ranks, after, tile=256):
    rows, width = d_pre_one.shape
    row = pl.BlockSpec((tile, width), lambda i: (i, 0))
    return pl.pallas_call(
        functools.partial(tokens_grad_kernel, parts=parts, ranks=ranks),
        grid=(rows // tile,),
        in_specs=[row] * 4 + [ANYWHERE] * (1 + len(after)),
        out_specs=row,
        out_shape=struct((rows, width)),
        scratch_shapes=[pltpu.VMEM((width, 3 * width), LOW), pltpu.SemaphoreType.DMA],
        compiler_params=params(40),
        cost_estimate=cost(6 * rows * width * width, 18 * rows * width),
        name="tokens_grad",
    )(d_pre_one, *grads, held, *after)


def swap(value, axis, bit):
    count = lax.axis_size(axis)
    return lax.ppermute(value, axis, [(at, at ^ (1 << bit)) for at in range(count)])


def bit_of(axis, bit):
    return (lax.axis_index(axis) // (1 << bit)) % 2


def pick_kernel(pick_ref, spot_ref, *refs, count):
    out_ref = refs[-1]
    for piece in range(count):

        @pl.when(pl.program_id(0) == piece)
        def _():
            out_ref[...] = refs[piece][...]


def pick(arrays, picks, spots, after):
    count = len(arrays)
    block = (1,) + arrays[0].shape[1:]
    rest = (0,) * (len(block) - 1)
    return pl.pallas_call(
        functools.partial(pick_kernel, count=count),
        grid_spec=pltpu.PrefetchScalarGridSpec(
            num_scalar_prefetch=2,
            grid=(count,),
            in_specs=[
                pl.BlockSpec(block, lambda i, picks, spots, at=at: (picks[at],) + rest)
                for at in range(count)
            ]
            + [ANYWHERE] * len(after),
            out_specs=pl.BlockSpec(block, lambda i, picks, spots: (spots[i],) + rest),
        ),
        out_shape=struct((count,) + block[1:]),
        compiler_params=params(40),
        cost_estimate=cost(0, 4 * count * math.prod(block)),
        name="pick",
    )(jnp.stack([jnp.int32(at) for at in picks]), spots, *arrays, *after)


def settle_kernel(side_ref, keep_ref, keep_far, came_ref, came_far, *refs):
    out_ref, send_ref = refs[-2:]
    send_ref[...] = (keep_far[...].astype(WIDE) + came_far[...].astype(WIDE)).astype(LOW)
    out_ref[...] = (keep_ref[...].astype(WIDE) + came_ref[...].astype(WIDE)).astype(LOW)


def settle(keep, came, side, after):
    half = keep.shape[0] // 2
    block = (1,) + keep.shape[1:]
    near = pl.BlockSpec(block, lambda i, side: (side[0] * half + i, 0, 0))
    far = pl.BlockSpec(block, lambda i, side: ((1 - side[0]) * half + i, 0, 0))
    out = pl.BlockSpec(block, lambda i, side: (i, 0, 0))
    return pl.pallas_call(
        settle_kernel,
        grid_spec=pltpu.PrefetchScalarGridSpec(
            num_scalar_prefetch=1,
            grid=(half,),
            in_specs=[near, far, near, far] + [ANYWHERE] * len(after),
            out_specs=[out, out],
        ),
        out_shape=[struct((half,) + keep.shape[1:])] * 2,
        compiler_params=params(40),
        cost_estimate=cost(0, 6 * math.prod(keep.shape)),
        name="settle",
    )(side, keep, keep, came, came, *after)


def plus_kernel(left_ref, right_ref, *refs):
    refs[-1][...] = (left_ref[...].astype(WIDE) + right_ref[...].astype(WIDE)).astype(LOW)


def plus(left, right, after):
    spec = pl.BlockSpec(left.shape, lambda i: (0, 0, 0))
    return pl.pallas_call(
        plus_kernel,
        grid=(1,),
        in_specs=[spec, spec] + [ANYWHERE] * len(after),
        out_specs=spec,
        out_shape=struct(left.shape),
        compiler_params=params(40),
        cost_estimate=cost(0, 6 * math.prod(left.shape)),
        name="plus",
    )(left, right, *after)


class Order:
    def __init__(self):
        self.after = ()

    def __call__(self, kernel, *args):
        out = kernel(*args, self.after)
        self.after = (out[-1] if isinstance(out, (tuple, list)) else out,)
        return out


class Reduce:
    def __init__(self, order, route, keep, send):
        self.order, self.route = order, list(route)
        self.keep = keep
        self.came = swap(send, "ctx", 0)

    def step(self):
        axis, bit = self.route.pop(0)
        if self.keep.shape[0] == 1:
            self.keep = self.order(plus, self.keep, self.came)
            self.came = swap(self.keep, axis, bit)
            return
        side = bit_of(axis, bit).reshape(1)
        self.keep, send = self.order(settle, self.keep, self.came, side)
        self.came = swap(send, axis, bit)

    def last(self):
        self.keep = self.order(plus, self.keep, self.came)
        return self.keep[0]


def both(value, axis, bit):
    other = swap(value, axis, bit)
    upper = bit_of(axis, bit) == 1
    return jnp.where(upper, other, value), jnp.where(upper, value, other)


class Sequences:
    def __init__(self, order, value):
        self.order, self.core, self.chip = order, bit_of("ctx", 0), bit_of("ctx", 1)
        self.blocks = value.reshape((4, value.shape[0] // 4) + value.shape[1:])
        send = lax.dynamic_slice_in_dim(self.blocks, 2 * (1 - self.chip), 2, 0)
        self.came = swap(send, "ctx", 1)

    def step(self):
        picks = (2 * self.chip + 1 - self.core, 1 - self.core)
        spots = jnp.arange(2, dtype=jnp.int32)
        self.late = swap(self.order(pick, (self.blocks, self.came), picks, spots), "ctx", 0)

    def last(self):
        arrays = (self.blocks, self.late, self.came, self.late)
        picks = (2 * self.chip + self.core, 0, self.core, 1)
        return self.order(pick, arrays, picks, jnp.arange(4, dtype=jnp.int32))


class Positions:
    def __init__(self, order, value):
        self.order, self.value = order, value
        spots = jnp.arange(2, dtype=jnp.int32)
        self.came = swap(order(pick, (value, value), (2, 3), spots), "ctx", 1)

    def step(self):
        spots = jnp.arange(2, dtype=jnp.int32)
        self.late = swap(self.order(pick, (self.value, self.came), (1, 1), spots), "ctx", 0)

    def last(self):
        arrays = (self.value, self.late, self.came, self.late)
        around = lax.axis_index("ctx") ^ jnp.arange(4, dtype=jnp.int32)
        return self.order(pick, arrays, (0, 0, 0, 1), around)


def packed(values, parts, order, columns):
    joined = jnp.concatenate(values, axis=1)
    length = joined.shape[1]
    bits = bits_of(parts)
    joined = joined.reshape((2,) * bits + (length,))
    joined = joined.transpose(tuple(bits - 1 - bit for bit in order) + (bits,))
    joined = jnp.pad(joined.reshape(parts, length), ((0, 0), (0, 2 * PAD * columns - length)))
    return joined.astype(LOW).reshape(parts, 2, PAD, columns)


def local(
    tokens,
    cotangent,
    input_weight,
    output_weight,
    up_weight,
    down_weight,
    query_bias,
    value_bias,
    output_bias,
    norm_gain,
    norm_shift,
    up_bias,
    down_bias,
    final_gain,
    final_shift,
):
    ranks, parts = lax.axis_size("ctx"), lax.axis_size("fsdp")
    rank = lax.axis_index("ctx")
    core = bit_of("ctx", 0)
    width = tokens.shape[2]

    bits = bits_of(parts)
    upward = tuple(range(bits))
    own, deep = input_weight.shape[0], down_weight.shape[0]
    half = width // 2

    order = Order()

    def columns_of(shard, index, count):
        count = shard.shape[1] // count
        return lax.dynamic_slice_in_dim(shard, index * count, count, 1)

    small = jnp.stack(
        [
            query_bias,
            value_bias,
            value_bias,
            output_bias,
            norm_gain,
            norm_shift,
            down_bias,
            final_gain,
            final_shift,
        ]
    )
    small = jnp.concatenate([small.reshape(-1), up_bias])[None]
    stages = []
    for bit in upward:
        small = jnp.concatenate(both(small, "fsdp", bit), axis=0)
        stages.append(small)
    vectors = small[:, : 9 * own].reshape(parts, 9, own).transpose(1, 0, 2).reshape(9, width)
    wide_up_bias = small[:, 9 * own :].reshape(1, -1)

    everyone = ("fsdp", "ctx")
    attn = lax.all_gather(columns_of(input_weight, rank, ranks), everyone, axis=0, tiled=False)
    held = lax.all_gather(
        jnp.concatenate(
            [
                columns_of(up_weight, rank, ranks),
                columns_of(output_weight, rank, ranks),
                lax.dynamic_slice_in_dim(down_weight, rank * (deep // ranks), deep // ranks, 0),
            ],
            axis=1,
        ),
        everyone,
        axis=0,
        tiled=False,
    )
    tok = Sequences(order, tokens)
    order.after = (stages[-1],)
    tok.step()
    tok = tok.last()
    cot = Sequences(order, cotangent)
    cot.step()
    cot = cot.last()
    shape = (ranks, tok.shape[1]) + tok.shape[2:]
    rows = math.prod(shape[:3])
    tok_rows, cot_rows = tok.reshape(rows, width), cot.reshape(rows, width)

    query, keys, values = order(merge, tok_rows, attn, vectors[0:3], parts, ranks)
    context = attend_forward(query, keys, values, shape).reshape(rows, width)
    (
        layer_out,
        hidden_low,
        active,
        d_branch,
        d_inner,
        d_attn,
        d_context,
        d_pre_one,
        sums,
        up_sums,
    ) = middle(context, tok_rows, cot_rows, held, vectors[1:9], wide_up_bias, parts, ranks)

    mine, other = core.reshape(1), (1 - core).reshape(1)
    row_vectors = sums[:6].reshape(6, parts, own).transpose(1, 0, 2).reshape(parts, 6 * own)
    order = Order()
    shards = [("fsdp", bit) for bit in upward]
    chip = [("ctx", 1)]
    turned = upward[1:2] + upward[:1] + upward[2:]

    down_mine, down_other, down_turn = down_grad(mine, active, d_branch, parts, turned, ())
    order.after = (down_other,)
    down_sum = Reduce(order, [("fsdp", bit) for bit in down_turn] + chip, down_mine, down_other)
    layer_out = Positions(order, layer_out.reshape(shape))
    up_mine, up_other = order(
        up_grad, mine, hidden_low, d_inner, parts, ranks, turned, width // ranks
    )
    down_sum.step()
    layer_out.step()
    up_mine, up_other = order(
        output_grad, mine, context, d_attn, up_mine, up_other, parts, ranks, turned
    )
    up_sum = Reduce(order, chip + [("fsdp", bit) for bit in turned], up_mine, up_other)
    up_sum.step()

    begun = ()
    for share in range(2 * shape[1]):
        begun = order(attend_backward, query, keys, values, d_context, shape, share, begun)[:5]
        if share == 0:
            layer_out = layer_out.last()
        if share == shape[1] - 1:
            down_sum.step()
    d_query, d_keys, d_values = [member.reshape(rows, width) for member in begun[:3]]
    down_sum.step()
    small_in = packed(
        [
            member.reshape(-1, 8, width)[:, 0].sum(axis=0).reshape(parts, own)
            for member in begun[3:]
        ]
        + [row_vectors, up_sums.reshape(parts, deep)],
        parts,
        upward,
        half,
    )

    near, far, near_keys, far_keys = order(
        input_grad, mine, tok_rows, d_query, d_values, d_keys, parts, ranks, upward
    )
    near, far = [
        lax.dynamic_update_slice(
            held,
            lax.dynamic_index_in_dim(small_in, side[0], 1, keepdims=False),
            (0, 2 * own, 0),
        )
        for held, side in ((near, mine), (far, other))
    ]
    input_sum = Reduce(order, shards + chip, near, far)
    keys_sum = Reduce(order, chip + shards, near_keys, far_keys)
    up_sum.step()
    input_sum.step()
    keys_sum.step()
    tokens_grad = order(
        tokens_grad_of, d_pre_one, (d_query, d_keys, d_values), attn, parts, ranks
    )
    tokens_grad = Positions(order, tokens_grad.reshape(shape))
    turns = [input_sum, keys_sum, up_sum, input_sum, down_sum, keys_sum, tokens_grad, up_sum]
    turns += [input_sum, keys_sum, down_sum, input_sum]
    for chain in turns:
        if not isinstance(chain, Reduce) or chain.route:
            chain.step()
    chains = [up_sum, down_sum, input_sum, keys_sum]
    while any(chain.route for chain in chains):
        for chain in chains:
            if chain.route:
                chain.step()
    up_done = up_sum.last()
    keys_done = keys_sum.last()
    down_done = down_sum.last()
    input_done = input_sum.last()
    tokens_grad = tokens_grad.last()
    layer_out, tokens_grad = [member.reshape(tokens.shape) for member in (layer_out, tokens_grad)]

    def across(value):
        lower, upper = both(jnp.stack(both(value, "ctx", 1)), "ctx", 0)
        return [lower[0], upper[0], lower[1], upper[1]]

    def joined(members):
        return jnp.concatenate(members, axis=1).astype(WIDE)

    lower, upper = both(down_done, "ctx", 0)
    down_result = jnp.concatenate([lower, upper], axis=0).astype(WIDE).T

    blocks = across(up_done)
    span = up_weight.shape[1] // ranks
    up_result = joined([member[:, :span] for member in blocks])
    output_result = joined([member[:, span:] for member in blocks])

    sides = both(input_done, "ctx", 0)
    query_result, value_result = [
        joined([side[at * own : (at + 1) * own] for side in sides]) for at in range(2)
    ]
    input_result = jnp.concatenate([query_result, joined(across(keys_done)), value_result], axis=1)
    flat = jnp.concatenate([side[2 * own :].reshape(-1) for side in sides]).astype(WIDE)
    eight = [flat[at * own : (at + 1) * own] for at in range(8)]
    up_bias_grad = flat[8 * own : 8 * own + deep]

    return (
        layer_out,
        tokens_grad,
        input_result,
        output_result,
        up_result,
        down_result,
        *eight[:5],
        up_bias_grad,
        *eight[5:],
    )


def solution(mesh):
    rows = P("fsdp", "ctx", None)
    matrix = P("fsdp", None)
    vector = P("fsdp")
    return jax.shard_map(
        local,
        mesh=mesh,
        in_specs=(rows,) * 2 + (matrix,) * 4 + (vector,) * 9,
        out_specs=(rows,) * 2 + (matrix,) * 4 + (vector,) * 9,
        check_vma=False,
    )
```

```python
import functools
import math

import jax
import jax.numpy as jnp
from jax import lax
from jax.experimental import pallas as pl
from jax.experimental.pallas import tpu as pltpu
from jax.sharding import PartitionSpec as P

HEAD = 64
EPSILON = 1e-05
LOW = jnp.bfloat16
WIDE = jnp.float32
NN = (((1,), (0,)), ((), ()))
NT = (((1,), (1,)), ((), ()))
TN = (((0,), (0,)), ((), ()))
PAD = 16


def dot(left, right, dims):
    return lax.dot_general(left, right, dims, preferred_element_type=WIDE)


def cost(flops, moved):
    scale = 16
    return pl.CostEstimate(
        flops=int(flops) // scale, bytes_accessed=int(moved) // scale, transcendentals=0
    )


def params(mib):
    return pltpu.CompilerParams(vmem_limit_bytes=mib << 20)


def struct(shape, dtype=LOW):
    return jax.ShapeDtypeStruct(tuple(shape), dtype)


def bits_of(size):
    return size.bit_length() - 1


ANYWHERE = pl.BlockSpec(memory_space=pl.ANY)


def placed(index, order):
    out = 0
    for bit in order:
        out = out * 2 + (index // 2**bit) % 2
    return out


def fetch(held_ref, parts, ranks, moves):
    for rank in range(ranks):

        def step(part, carry):
            for first, place, sem in moves:
                target = place(part, rank)
                source = held_ref.at[part * ranks + rank].at[:, pl.ds(first, target.shape[1])]
                pltpu.make_async_copy(source, target, sem).start()
            return carry

        lax.fori_loop(0, parts, step, 0)


def landed(target, sem):
    pltpu.make_async_copy(target, target, sem).wait()


def ds(index, size):
    return pl.ds(pl.multiple_of(index * size, size), size)


def fetch_input(held_ref, weight, sem, parts, ranks):
    width = weight.shape[0]
    rows, columns = width // parts, 3 * width // ranks

    def place(part, rank):
        return weight.at[ds(part, rows), pl.ds(rank * columns, columns)]

    fetch(held_ref, parts, ranks, [(0, place, sem)])
    landed(weight, sem)


def merge_kernel(tok_ref, bias_ref, held_ref, *refs, parts, ranks):
    q_ref, k_ref, v_ref, weight, sem = refs[-5:]
    width = tok_ref.shape[1]

    @pl.when(pl.program_id(0) == 0)
    def _():
        fetch_input(held_ref, weight, sem, parts, ranks)

    rows = tok_ref[...]
    for at, out in enumerate((q_ref, k_ref, v_ref)):
        value = dot(rows, weight[:, at * width : (at + 1) * width], NN)
        if at != 1:
            value = value + bias_ref[at : at + 1, :].astype(WIDE)
        out[...] = value.astype(LOW)


def merge(tok, held, bias, parts, ranks, after, tile=256):
    rows, width = tok.shape
    row = pl.BlockSpec((tile, width), lambda i: (i, 0))
    return pl.pallas_call(
        functools.partial(merge_kernel, parts=parts, ranks=ranks),
        grid=(rows // tile,),
        in_specs=[row, pl.BlockSpec(bias.shape, lambda i: (0, 0))]
        + [ANYWHERE] * (1 + len(after)),
        out_specs=[row] * 3,
        out_shape=[struct(tok.shape)] * 3,
        scratch_shapes=[pltpu.VMEM((width, 3 * width), LOW), pltpu.SemaphoreType.DMA],
        compiler_params=params(60),
        cost_estimate=cost(6 * rows * width * width, 14 * rows * width),
        name="merge",
    )(tok, bias, held, *after)


def attend_forward_kernel(q_ref, k_ref, v_ref, o_ref):
    shape = o_ref.shape
    query, keys, values = [ref[...].reshape(-1, 2 * HEAD) for ref in (q_ref, k_ref, v_ref)]
    first = lax.broadcasted_iota(jnp.int32, query.shape, 1) < HEAD
    zero = jnp.zeros_like(query)
    outs = []
    for one in (jnp.where(first, query, zero), jnp.where(first, zero, query)):
        scores = dot(one, keys, NT)
        peak = jnp.max(scores, axis=1, keepdims=True)
        raised = jnp.exp((scores - peak) * (1.0 / math.sqrt(HEAD)))
        total = jnp.sum(raised, axis=1, keepdims=True)
        outs.append(dot(raised.astype(LOW), values, NN) * (1.0 / total))
    o_ref[...] = jnp.where(first, outs[0], outs[1]).astype(LOW).reshape(shape)


def head_spec(shape):
    pieces, _, length, _ = shape
    return pl.BlockSpec((pieces, 1, length, 2 * HEAD), lambda s, h: (0, s, 0, h))


def attend_forward(query, keys, values, shape):
    spec = head_spec(shape)
    rows = math.prod(shape[:3])
    area = rows * shape[0] * shape[2] * shape[3]
    return pl.pallas_call(
        attend_forward_kernel,
        grid=(shape[1], shape[3] // (2 * HEAD)),
        in_specs=[spec] * 3,
        out_specs=spec,
        out_shape=struct(shape),
        compiler_params=params(60),
        cost_estimate=cost(16 * area, 8 * rows * shape[3]),
        name="attend_forward",
    )(*[member.reshape(shape) for member in (query, keys, values)])


def attend_backward_kernel(q_ref, k_ref, v_ref, c_ref, *refs):
    dq_ref, dk_ref, dv_ref, qs_ref, vs_ref, mark_ref = refs[-6:]
    mark_ref[...] = jnp.zeros_like(mark_ref)
    shape = dq_ref.shape
    query, keys, values, d_context = [
        ref[...].reshape(-1, 2 * HEAD) for ref in (q_ref, k_ref, v_ref, c_ref)
    ]
    first = lax.broadcasted_iota(jnp.int32, query.shape, 1) < HEAD
    zero = jnp.zeros_like(query)
    factor = 1.0 / math.sqrt(HEAD)
    outs = []
    for head in range(2):

        def only(value):
            return jnp.where(first, value, zero) if head == 0 else jnp.where(first, zero, value)

        scores = dot(keys, only(query), NT)
        peak = jnp.max(scores, axis=0, keepdims=True)
        raised = jnp.exp((scores - peak) * factor)
        probs = raised * (1.0 / jnp.sum(raised, axis=0, keepdims=True))
        d_probs = dot(values, only(d_context), NT)
        product = probs * d_probs
        d_scores = (product - probs * jnp.sum(product, axis=0, keepdims=True)).astype(LOW)
        outs.append(
            (
                dot(d_scores, keys, TN),
                dot(d_scores, query, NN),
                dot(probs.astype(LOW), d_context, NN),
            )
        )
    d_query = (jnp.where(first, outs[0][0], outs[1][0]) * factor).astype(LOW)
    d_keys = (jnp.where(first, outs[0][1], outs[1][1]) * factor).astype(LOW)
    d_values = jnp.where(first, outs[0][2], outs[1][2]).astype(LOW)
    dq_ref[...] = d_query.reshape(shape)
    dk_ref[...] = d_keys.reshape(shape)
    dv_ref[...] = d_values.reshape(shape)
    for value, out in ((d_query, qs_ref), (d_values, vs_ref)):
        total = jnp.sum(value.astype(WIDE), axis=0, keepdims=True)
        out[...] = jnp.broadcast_to(total, (8, 2 * HEAD))


def attend_backward(query, keys, values, d_context, shape, share, begun, after):
    pieces, count, length, width = shape
    pairs = width // (2 * HEAD) // 2
    sequence, first = share // 2, share % 2 * pairs
    spec = pl.BlockSpec((pieces, 1, length, 2 * HEAD), lambda h: (0, sequence, 0, first + h))
    sums = pl.BlockSpec((8, 2 * HEAD), lambda h: (sequence, first + h))
    rows = math.prod(shape[:3])
    area = rows * pieces * length * width // count // 2
    return pl.pallas_call(
        attend_backward_kernel,
        grid=(pairs,),
        in_specs=[spec] * 4 + [ANYWHERE] * (len(begun) + len(after)),
        out_specs=[spec] * 3 + [sums] * 2 + [pl.BlockSpec((8, 2 * HEAD), lambda h: (0, 0))],
        out_shape=[struct(shape)] * 3
        + [struct((8 * count, width), WIDE)] * 2
        + [struct((8, 2 * HEAD), WIDE)],
        input_output_aliases={4 + at: at for at in range(len(begun))},
        compiler_params=params(60),
        cost_estimate=cost(40 * area, 14 * rows * width // count),
        name="attend_backward",
    )(*[member.reshape(shape) for member in (query, keys, values, d_context)], *begun, *after)


def gelu_and_slope(value):
    raised = jnp.exp(value * value * -0.5)
    at = 1.0 / (1.0 + (0.3275911 * math.sqrt(0.5)) * jnp.abs(value))
    series = 0.5 * -1.453152027 + at * (0.5 * 1.061405429)
    for term in (1.421413741, -0.284496736, 0.254829592):
        series = 0.5 * term + at * series
    tail = at * series * raised
    below = jnp.where(value >= 0, 1.0 - tail, tail)
    return value * below, below + value * raised * (1.0 / math.sqrt(2.0 * math.pi))


def mean(value):
    return jnp.mean(value, axis=1, keepdims=True)


def total(value):
    return jnp.sum(value, axis=0, keepdims=True)


def norm_forward(value):
    centre = value - mean(value)
    inverse = lax.rsqrt(mean(centre * centre) + EPSILON)
    return centre * inverse, inverse


def norm_backward(upstream, normed, inverse, gain):
    scaled = upstream * gain
    return inverse * (scaled - mean(scaled) - normed * mean(scaled * normed))


def middle_kernel(
    context_ref,
    tok_ref,
    cot_ref,
    vector_ref,
    up_bias_ref,
    *refs,
    parts,
    ranks,
    chunk,
):
    held_ref, refs = refs[0], refs[-15:]
    (
    out_ref,
    hidden_ref,
    active_ref,
    d_branch_ref,
    d_inner_ref,
    d_attn_ref,
    d_context_ref,
    d_pre_ref,
    sums_ref,
    up_sums_ref,
    output_weight,
    up_weight,
    down_weight,
    slope_ref,
    sems,
    ) = refs
    width, inner_width = up_weight.shape
    start = pl.program_id(0) == 0

    @pl.when(start)
    def _():
        own = width // parts
        span, narrow = inner_width // ranks, width // ranks
        fetch(
            held_ref,
            parts,
            ranks,
            [
                (
                    span,
                    lambda part, rank: output_weight.at[
                        ds(part, own), pl.ds(rank * narrow, narrow)
                    ],
                    sems.at[0],
                ),
                (
                    0,
                    lambda part, rank: up_weight.at[ds(part, own), pl.ds(rank * span, span)],
                    sems.at[1],
                ),
                (
                    span + narrow,
                    lambda part, rank: down_weight.at[ds(part * ranks + rank, own), :],
                    sems.at[2],
                ),
            ],
        )
        sums_ref[...] = jnp.zeros_like(sums_ref)
        up_sums_ref[...] = jnp.zeros_like(up_sums_ref)
        landed(output_weight, sems.at[0])

    output_bias, norm_gain, norm_shift, down_bias, final_gain, final_shift = [
        vector_ref[at : at + 1, :].astype(WIDE) for at in range(2, 8)
    ]
    pre_one = (
        tok_ref[...].astype(WIDE) + dot(context_ref[...], output_weight[...], NN) + output_bias
    )
    normed_one, inverse_one = norm_forward(pre_one)
    hidden = normed_one * norm_gain + norm_shift
    hidden_low = hidden.astype(LOW)
    hidden_ref[...] = hidden_low

    @pl.when(start)
    def _():
        landed(up_weight, sems.at[1])
        landed(down_weight, sems.at[2])

    branch = hidden + down_bias
    for at in range(0, inner_width, chunk):
        span = slice(at, at + chunk)
        inner = dot(hidden_low, up_weight[:, span], NN) + up_bias_ref[:, span].astype(WIDE)
        active, slope = gelu_and_slope(inner)
        active = active.astype(LOW)
        active_ref[:, span] = active
        slope_ref[:, span] = slope
        branch = branch + dot(active, down_weight[span, :], NN)
    normed_two, inverse_two = norm_forward(branch)
    out_ref[...] = (normed_two * final_gain + final_shift).astype(LOW)
    upstream = cot_ref[...].astype(WIDE)
    d_pre_two = norm_backward(upstream, normed_two, inverse_two, final_gain)
    d_branch = d_pre_two.astype(LOW)
    d_branch_ref[...] = d_branch
    d_hidden = d_pre_two
    for at in range(0, inner_width, chunk):
        span = slice(at, at + chunk)
        d_inner = (dot(d_branch, down_weight[span, :], NT) * slope_ref[:, span]).astype(LOW)
        d_inner_ref[:, span] = d_inner
        up_sums_ref[:, span] += total(d_inner.astype(WIDE))
        d_hidden = d_hidden + dot(d_inner, up_weight[:, span], NT)
    d_pre_one = norm_backward(d_hidden, normed_one, inverse_one, norm_gain)
    d_attn = d_pre_one.astype(LOW)
    d_attn_ref[...] = d_attn
    d_pre_ref[...] = d_pre_one
    d_context_ref[...] = dot(d_attn, output_weight[...], NT).astype(LOW)
    sums = (
        d_pre_one,
        d_hidden * normed_one,
        d_hidden,
        d_pre_two,
        upstream * normed_two,
        upstream,
    )
    for at, value in enumerate(sums):
        sums_ref[at : at + 1, :] += total(value)


def middle(context, tok, cot, held, vectors, up_bias, parts, ranks, tile=256):
    rows, width = tok.shape
    inner_width = up_bias.shape[1]
    row = pl.BlockSpec((tile, width), lambda i: (i, 0))
    broad = pl.BlockSpec((tile, inner_width), lambda i: (i, 0))

    def whole(shape):
        return pl.BlockSpec(shape, lambda i: (0, 0))

    low, deep = struct((rows, width)), struct((rows, inner_width))
    return pl.pallas_call(
        functools.partial(middle_kernel, parts=parts, ranks=ranks, chunk=1024),
        grid=(rows // tile,),
        in_specs=[row] * 3 + [whole(vectors.shape), whole(up_bias.shape), ANYWHERE],
        out_specs=[row, row, broad, row, broad, row, row, row]
        + [whole((8, width)), whole((1, inner_width))],
        scratch_shapes=[
            pltpu.VMEM((width, width), LOW),
            pltpu.VMEM((width, inner_width), LOW),
            pltpu.VMEM((inner_width, width), LOW),
            pltpu.VMEM((tile, inner_width), WIDE),
            pltpu.SemaphoreType.DMA((3,)),
        ],
        out_shape=[low, low, deep, low, deep, low, low, struct((rows, width), WIDE)]
        + [struct((8, width), WIDE), struct((1, inner_width), WIDE)],
        compiler_params=params(60),
        cost_estimate=cost(
            4 * rows * width * (2 * inner_width + width), 18 * width * inner_width * rows // 1024
        ),
        name="middle",
    )(context, tok, cot, vectors, up_bias, held)


def down_grad_kernel(half_ref, near_ref, far_ref, active_ref, *refs):
    out_near, *out_far, turned = refs[-4:]
    columns = near_ref.shape[1]

    @pl.when(pl.program_id(0) == 0)
    def _():
        turned[:columns] = near_ref[...].T
        turned[columns:] = far_ref[...].T

    group, _, _, deep = out_near.shape
    result = dot(turned[...], active_ref[...], NN).astype(LOW)
    for part in range(group):
        at = placed(part, range(bits_of(group)))
        span = slice(part * deep, (part + 1) * deep)
        out_near[at, 0] = result[:columns, span]
        out_far[at // (group // 2)][at % (group // 2), 0] = result[columns:, span]


def down_grad(half, active, d_branch, parts, order, after):
    rows, inner_width = active.shape
    columns = d_branch.shape[1] // 2
    deep = inner_width // parts
    group = max(2, 1024 // deep)
    steps = parts // group
    low = bits_of(group)
    order = tuple(range(low)) + tuple(bit for bit in order if bit >= low)
    high = [bit - low for bit in order[low:]]

    def spec(count):
        return pl.BlockSpec((count, 1, columns, deep), lambda i, half: (0, placed(i, high), 0, 0))

    near, *far = pl.pallas_call(
        down_grad_kernel,
        grid_spec=pltpu.PrefetchScalarGridSpec(
            num_scalar_prefetch=1,
            grid=(steps,),
            in_specs=[
                pl.BlockSpec((rows, columns), lambda i, half: (0, half[0])),
                pl.BlockSpec((rows, columns), lambda i, half: (0, 1 - half[0])),
                pl.BlockSpec((rows, group * deep), lambda i, half: (0, i)),
            ]
            + [ANYWHERE] * len(after),
            out_specs=[spec(group), spec(group // 2), spec(group // 2)],
            scratch_shapes=[pltpu.VMEM((2 * columns, rows), LOW)],
        ),
        out_shape=[struct((group, steps, columns, deep))]
        + [struct((group // 2, steps, columns, deep))] * 2,
        compiler_params=params(60),
        cost_estimate=cost(4 * rows * inner_width * columns, 4 * rows * inner_width),
        name="down_grad",
    )(half, d_branch, d_branch, active, *after)
    return near.reshape(parts, columns, deep), [
        member.reshape(parts // 2, columns, deep) for member in far
    ], order


def spread(result, outs, order):
    parts = 2 ** len(order)
    rows, each = result.shape[0] // parts, parts // len(outs)
    for part in range(parts):
        at = placed(part, order)
        outs[at // each][at % each] = result[part * rows : (part + 1) * rows]


def output_grad_kernel(half_ref, context_ref, *refs, order, chips):
    grads, outs, turned = refs[:2], refs[-chips - 2 : -1], refs[-1]
    at = pl.program_id(0)

    @pl.when(at == 0)
    def _():
        turned[...] = context_ref[...].T

    for step in range(2 * chips):

        @pl.when(at == step)
        def _():
            result = dot(turned[...], grads[step // chips][...], NN).astype(LOW)
            spread(result, [outs[min(step, chips)].at[0]], order)


def output_grad(half, context, d_attn, near, far, parts, ranks, order, after):
    rows, width = context.shape
    chips, narrow, own = ranks // 2, width // ranks, width // parts
    shape = (1, parts, own, near.shape[2])
    last = shape[3] // narrow - 1
    block = (1, parts, own, narrow)

    def far_at(i):
        return jnp.minimum(i, chips - 1)

    def near_at(i):
        return jnp.maximum(i - chips, 0)

    near_shape = (chips,) + shape[1:]
    *far, near = pl.pallas_call(
        functools.partial(output_grad_kernel, order=order, chips=chips),
        grid_spec=pltpu.PrefetchScalarGridSpec(
            num_scalar_prefetch=1,
            grid=(ranks,),
            in_specs=[
                pl.BlockSpec((rows, width), lambda i, half: (0, 0)),
                pl.BlockSpec((rows, narrow), lambda i, half: (0, 2 * far_at(i) + 1 - half[0])),
                pl.BlockSpec((rows, narrow), lambda i, half: (0, 2 * near_at(i) + half[0])),
            ]
            + [ANYWHERE] * (1 + chips + len(after)),
            out_specs=[pl.BlockSpec(block, lambda i, half: (0, 0, 0, last))] * chips
            + [pl.BlockSpec(block, lambda i, half: (near_at(i), 0, 0, last))],
            scratch_shapes=[pltpu.VMEM((width, rows), LOW)],
        ),
        out_shape=[struct(shape)] * chips + [struct(near_shape)],
        input_output_aliases={4 + at: at for at in range(chips + 1)},
        compiler_params=params(60),
        cost_estimate=cost(2 * rows * width * width, 6 * rows * width),
        name="output_grad",
    )(
        half,
        context,
        d_attn,
        d_attn,
        *[member.reshape(shape) for member in far],
        near.reshape(near_shape),
        *after,
    )
    return near.reshape(-1, own, shape[3]), [member[0] for member in far]


def up_grad_kernel(half_ref, hidden_ref, grad_ref, *refs, order, chips):
    outs, turned = refs[-chips - 2 : -1], refs[-1]
    at = pl.program_id(0)

    @pl.when(at == 0)
    def _():
        turned[...] = hidden_ref[...].T

    for step in range(2 * chips):

        @pl.when(at == step)
        def _():
            result = dot(turned[...], grad_ref[...], NN).astype(LOW)
            spread(result, [outs[min(step, chips)].at[0]], order)


def up_grad(half, hidden_low, d_inner, parts, ranks, order, extra, after):
    rows, width = hidden_low.shape
    columns = d_inner.shape[1] // ranks
    chips = ranks // 2

    def column(i, half):
        far = i < chips
        return 0, jnp.where(far, 2 * i + 1 - half[0], 2 * (i - chips) + half[0])

    block = (1, parts, width // parts, columns)
    shape = block[1:3] + (columns + extra,)
    *far, near = pl.pallas_call(
        functools.partial(up_grad_kernel, order=order, chips=chips),
        grid_spec=pltpu.PrefetchScalarGridSpec(
            num_scalar_prefetch=1,
            grid=(ranks,),
            in_specs=[
                pl.BlockSpec((rows, width), lambda i, half: (0, 0)),
                pl.BlockSpec((rows, columns), column),
            ]
            + [ANYWHERE] * len(after),
            out_specs=[pl.BlockSpec(block, lambda i, half: (0, 0, 0, 0))] * chips
            + [pl.BlockSpec(block, lambda i, half: (jnp.maximum(i - chips, 0), 0, 0, 0))],
            scratch_shapes=[pltpu.VMEM((width, rows), LOW)],
        ),
        out_shape=[struct((1,) + shape)] * chips + [struct((chips,) + shape)],
        compiler_params=params(60),
        cost_estimate=cost(2 * rows * width * columns * ranks, 4 * rows * columns * ranks),
        name="up_grad",
    )(half, hidden_low, d_inner, *after)
    return near.reshape((-1,) + shape[1:]), [member[0] for member in far]


def input_grad_kernel(half_ref, tok_ref, *refs, orders):
    grads, turned = refs[:6], refs[-1]
    far_low, far_high, far_keys, near, near_keys = refs[-6:-1]
    outs = [far_low, far_high], [far_keys], [near], [near_keys]
    at = pl.program_id(0)

    @pl.when(at == 0)
    def _():
        turned[...] = tok_ref[...].T

    for step in range(6):

        @pl.when(at == step)
        def _():
            result = dot(turned[...], grads[step][...], NN).astype(LOW)
            keys = step % 3 == 2
            spread(result, outs[step // 3 * 2 + keys], orders[keys])


def input_grad(half, tok, d_query, d_values, d_keys, parts, orders, after):
    rows, width = tok.shape
    columns, own = width // 2, width // parts
    deep = 2 * own + PAD
    ins = []
    for side in range(2):

        def column(i, half, side=side):
            return 0, half[0] if side else 1 - half[0]

        ins += [pl.BlockSpec((rows, columns), column)] * 3

    def spec(count, side):
        return pl.BlockSpec(
            (count, own, columns), lambda i, half: (0, jnp.clip(i - 3 * side, 0, 1), 0)
        )

    keys = pl.BlockSpec((parts, own, columns), lambda i, half: (0, 0, 0))
    far_low, far_high, far_keys, near, near_keys = pl.pallas_call(
        functools.partial(input_grad_kernel, orders=orders),
        grid_spec=pltpu.PrefetchScalarGridSpec(
            num_scalar_prefetch=1,
            grid=(6,),
            in_specs=[pl.BlockSpec((rows, width), lambda i, half: (0, 0))]
            + ins
            + [ANYWHERE] * len(after),
            out_specs=[spec(parts // 2, 0), spec(parts // 2, 0), keys, spec(parts, 1), keys],
            scratch_shapes=[pltpu.VMEM((width, rows), LOW)],
        ),
        out_shape=[
            struct((parts // 2, deep, columns)),
            struct((parts // 2, deep, columns)),
            struct((parts, own, columns)),
            struct((parts, deep, columns)),
            struct((parts, own, columns)),
        ],
        compiler_params=params(60),
        cost_estimate=cost(6 * rows * width * width, 10 * rows * width),
        name="input_grad",
    )(half, tok, *[d_query, d_values, d_keys] * 2, *after)
    return near, [far_low, far_high], near_keys, far_keys


def tokens_grad_kernel(d_pre_ref, dq_ref, dk_ref, dv_ref, held_ref, *refs, parts, ranks):
    out_ref, weight, sem = refs[-3:]
    width = d_pre_ref.shape[1]

    @pl.when(pl.program_id(0) == 0)
    def _():
        fetch_input(held_ref, weight, sem, parts, ranks)

    value = d_pre_ref[...]
    for at, ref in enumerate((dq_ref, dk_ref, dv_ref)):
        value = value + dot(ref[...], weight[:, at * width : (at + 1) * width], NT)
    out_ref[...] = value.astype(LOW)


def tokens_grad_of(d_pre_one, grads, held, parts, ranks, after, tile=256):
    rows, width = d_pre_one.shape
    row = pl.BlockSpec((tile, width), lambda i: (i, 0))
    return pl.pallas_call(
        functools.partial(tokens_grad_kernel, parts=parts, ranks=ranks),
        grid=(rows // tile,),
        in_specs=[row] * 4 + [ANYWHERE] * (1 + len(after)),
        out_specs=row,
        out_shape=struct((rows, width)),
        scratch_shapes=[pltpu.VMEM((width, 3 * width), LOW), pltpu.SemaphoreType.DMA],
        compiler_params=params(60),
        cost_estimate=cost(6 * rows * width * width, 18 * rows * width),
        name="tokens_grad",
    )(d_pre_one, *grads, held, *after)


def swap(value, axis, bit):
    count = lax.axis_size(axis)
    return lax.ppermute(value, axis, [(at, at ^ (1 << bit)) for at in range(count)])


def bit_of(axis, bit):
    return (lax.axis_index(axis) // (1 << bit)) % 2


def pick_kernel(pick_ref, spot_ref, *refs, count):
    out_ref = refs[-1]
    for piece in range(count):

        @pl.when(pl.program_id(0) == piece)
        def _():
            out_ref[...] = refs[piece][...]


def pick(arrays, picks, spots, after):
    count = len(arrays)
    block = (1,) + arrays[0].shape[1:]
    rest = (0,) * (len(block) - 1)
    return pl.pallas_call(
        functools.partial(pick_kernel, count=count),
        grid_spec=pltpu.PrefetchScalarGridSpec(
            num_scalar_prefetch=2,
            grid=(count,),
            in_specs=[
                pl.BlockSpec(block, lambda i, picks, spots, at=at: (picks[at],) + rest)
                for at in range(count)
            ]
            + [ANYWHERE] * len(after),
            out_specs=pl.BlockSpec(block, lambda i, picks, spots: (spots[i],) + rest),
        ),
        out_shape=struct((count,) + block[1:]),
        compiler_params=params(40),
        cost_estimate=cost(0, 4 * count * math.prod(block)),
        name="pick",
    )(jnp.stack([jnp.int32(at) for at in picks]), spots, *arrays, *after)


def settle_kernel(side_ref, keep_ref, keep_far, low_ref, high_ref, *refs, swapped):
    out_ref, send_ref = refs[-2:]

    def add(near, far):
        send_ref[...] = (keep_far[...].astype(WIDE) + far[...].astype(WIDE)).astype(LOW)
        out_ref[...] = (keep_ref[...].astype(WIDE) + near[...].astype(WIDE)).astype(LOW)

    if not swapped:
        add(low_ref, high_ref)
        return

    @pl.when(side_ref[0] == 0)
    def _():
        add(low_ref, high_ref)

    @pl.when(side_ref[0] == 1)
    def _():
        add(high_ref, low_ref)


def settle(keep, came, side, after):
    half = keep.shape[0] // 2
    block = (1,) + keep.shape[1:]
    near = pl.BlockSpec(block, lambda i, side: (side[0] * half + i, 0, 0))
    far = pl.BlockSpec(block, lambda i, side: ((1 - side[0]) * half + i, 0, 0))
    out = pl.BlockSpec(block, lambda i, side: (i, 0, 0))
    whole = len(came) == 1
    return pl.pallas_call(
        functools.partial(settle_kernel, swapped=not whole),
        grid_spec=pltpu.PrefetchScalarGridSpec(
            num_scalar_prefetch=1,
            grid=(half,),
            in_specs=[near, far] + ([near, far] if whole else [out, out]) + [ANYWHERE] * len(after),
            out_specs=[out, out],
        ),
        out_shape=[struct((half,) + keep.shape[1:])] * 2,
        compiler_params=params(60 if 2 * math.prod(keep.shape) > 3 << 20 else 40),
        cost_estimate=cost(0, 6 * math.prod(keep.shape)),
        name="settle",
    )(side, keep, keep, *(came * 2 if whole else came), *after)


def plus_kernel(left_ref, right_ref, *refs):
    refs[-1][...] = (left_ref[...].astype(WIDE) + right_ref[...].astype(WIDE)).astype(LOW)


def plus(left, right, after):
    spec = pl.BlockSpec(left.shape, lambda i: (0, 0, 0))
    return pl.pallas_call(
        plus_kernel,
        grid=(1,),
        in_specs=[spec, spec] + [ANYWHERE] * len(after),
        out_specs=spec,
        out_shape=struct(left.shape),
        compiler_params=params(40),
        cost_estimate=cost(0, 6 * math.prod(left.shape)),
        name="plus",
    )(left, right, *after)


class Order:
    def __init__(self):
        self.after = ()

    def __call__(self, kernel, *args):
        out = kernel(*args, self.after)
        self.after = (out[-1] if isinstance(out, (tuple, list)) else out,)
        return out


class Reduce:
    def __init__(self, order, route, keep, *send):
        self.order, self.route = order, list(route)
        self.keep = keep
        self.came = [swap(member, "ctx", 0) for member in send]

    def step(self):
        axis, bit = self.route.pop(0)
        if self.keep.shape[0] == 1:
            self.keep = send = self.order(plus, self.keep, self.came[0])
        else:
            side = bit_of(axis, bit).reshape(1)
            self.keep, send = self.order(settle, self.keep, self.came, side)
        self.came = [swap(send, axis, bit)]

    def last(self):
        return self.order(plus, self.keep, self.came[0])[0]


def both(value, axis, bit):
    other = swap(value, axis, bit)
    upper = bit_of(axis, bit) == 1
    return jnp.where(upper, other, value), jnp.where(upper, value, other)


class Sequences:
    def __init__(self, order, value):
        self.order, self.core, self.chip = order, bit_of("ctx", 0), bit_of("ctx", 1)
        self.blocks = value.reshape((4, value.shape[0] // 4) + value.shape[1:])
        send = lax.dynamic_slice_in_dim(self.blocks, 2 * (1 - self.chip), 2, 0)
        self.came = swap(send, "ctx", 1)

    def step(self):
        picks = (2 * self.chip + 1 - self.core, 1 - self.core)
        spots = jnp.arange(2, dtype=jnp.int32)
        self.late = swap(self.order(pick, (self.blocks, self.came), picks, spots), "ctx", 0)

    def last(self):
        arrays = (self.blocks, self.late, self.came, self.late)
        picks = (2 * self.chip + self.core, 0, self.core, 1)
        return self.order(pick, arrays, picks, jnp.arange(4, dtype=jnp.int32))


class Positions:
    def __init__(self, order, value):
        self.order, self.value = order, value
        send = order(pick, (value, value), (1, 3), jnp.arange(2, dtype=jnp.int32))
        self.came = swap(send, "ctx", 0)

    def step(self):
        spots = jnp.arange(2, dtype=jnp.int32)
        send = self.order(pick, (self.value, self.came), (2, 1), spots)
        self.late = swap(send, "ctx", 1)

    def last(self):
        around = lax.axis_index("ctx") ^ jnp.arange(4, dtype=jnp.int32)
        arrays = (self.value, self.came, self.late, self.late)
        return self.order(pick, arrays, (0, 0, 0, 1), around)


def packed(values, parts, order, columns):
    joined = jnp.concatenate(values, axis=1)
    length = joined.shape[1]
    bits = bits_of(parts)
    joined = joined.reshape((2,) * bits + (length,))
    joined = joined.transpose(tuple(bits - 1 - bit for bit in order) + (bits,))
    joined = jnp.pad(joined.reshape(parts, length), ((0, 0), (0, 2 * PAD * columns - length)))
    return joined.astype(LOW).reshape(parts, 2, PAD, columns)


def local(
    tokens,
    cotangent,
    input_weight,
    output_weight,
    up_weight,
    down_weight,
    query_bias,
    value_bias,
    output_bias,
    norm_gain,
    norm_shift,
    up_bias,
    down_bias,
    final_gain,
    final_shift,
):
    ranks, parts = lax.axis_size("ctx"), lax.axis_size("fsdp")
    rank = lax.axis_index("ctx")
    core = bit_of("ctx", 0)
    width = tokens.shape[2]

    bits = bits_of(parts)
    upward = tuple(range(bits))
    own, deep = input_weight.shape[0], down_weight.shape[0]
    half = width // 2

    order = Order()

    def columns_of(shard, index, count):
        count = shard.shape[1] // count
        return lax.dynamic_slice_in_dim(shard, index * count, count, 1)

    small = jnp.stack(
        [
            query_bias,
            value_bias,
            value_bias,
            output_bias,
            norm_gain,
            norm_shift,
            down_bias,
            final_gain,
            final_shift,
        ]
    )
    small = jnp.concatenate([small.reshape(-1), up_bias])[None]
    stages = []
    for bit in upward:
        small = jnp.concatenate(both(small, "fsdp", bit), axis=0)
        stages.append(small)
    vectors = small[:, : 9 * own].reshape(parts, 9, own).transpose(1, 0, 2).reshape(9, width)
    wide_up_bias = small[:, 9 * own :].reshape(1, -1)

    everyone = ("fsdp", "ctx")
    attn = lax.all_gather(columns_of(input_weight, rank, ranks), everyone, axis=0, tiled=False)
    held = lax.all_gather(
        jnp.concatenate(
            [
                columns_of(up_weight, rank, ranks),
                columns_of(output_weight, rank, ranks),
                lax.dynamic_slice_in_dim(down_weight, rank * (deep // ranks), deep // ranks, 0),
            ],
            axis=1,
        ),
        everyone,
        axis=0,
        tiled=False,
    )
    tok = Sequences(order, tokens)
    order.after = (stages[-1],)
    tok.step()
    tok = tok.last()
    cot = Sequences(order, cotangent)
    cot.step()
    cot = cot.last()
    shape = (ranks, tok.shape[1]) + tok.shape[2:]
    rows = math.prod(shape[:3])
    tok_rows, cot_rows = tok.reshape(rows, width), cot.reshape(rows, width)

    query, keys, values = order(merge, tok_rows, attn, vectors[0:3], parts, ranks)
    context = attend_forward(query, keys, values, shape).reshape(rows, width)
    (
        layer_out,
        hidden_low,
        active,
        d_branch,
        d_inner,
        d_attn,
        d_context,
        d_pre_one,
        sums,
        up_sums,
    ) = middle(context, tok_rows, cot_rows, held, vectors[1:9], wide_up_bias, parts, ranks)

    mine, other = core.reshape(1), (1 - core).reshape(1)
    row_vectors = sums[:6].reshape(6, parts, own).transpose(1, 0, 2).reshape(parts, 6 * own)
    order = Order()
    shards = [("fsdp", bit) for bit in upward]
    chip = [("ctx", 1)]
    turned = upward[1:2] + upward[:1] + upward[2:]

    up_mine, up_other = up_grad(
        mine, hidden_low, d_inner, parts, ranks, upward, width // ranks, ()
    )
    up_mine, up_other = output_grad(
        mine, context, d_attn, up_mine, up_other, parts, ranks, upward, ()
    )
    order.after = (up_mine,)
    up_sum = Reduce(order, chip + shards, up_mine, *up_other)
    down_mine, down_other, down_turn = order(down_grad, mine, active, d_branch, parts, upward)
    order.after = (down_mine,)
    down_sum = Reduce(
        order, [("fsdp", bit) for bit in down_turn] + chip, down_mine, *down_other
    )
    up_sum.step()
    down_sum.step()

    layer_out = Positions(order, layer_out.reshape(shape))
    begun = ()
    for share in range(2 * shape[1]):
        begun = order(attend_backward, query, keys, values, d_context, shape, share, begun)[:5]
    d_query, d_keys, d_values = [member.reshape(rows, width) for member in begun[:3]]
    up_sum.step()
    down_sum.step()
    tokens_grad = order(
        tokens_grad_of, d_pre_one, (d_query, d_keys, d_values), attn, parts, ranks
    )
    tokens_grad = Positions(order, tokens_grad.reshape(shape))
    small_in = packed(
        [
            member.reshape(-1, 8, width)[:, 0].sum(axis=0).reshape(parts, own)
            for member in begun[3:]
        ]
        + [row_vectors, up_sums.reshape(parts, deep)],
        parts,
        upward,
        half,
    )

    orders = upward, turned
    near, far, near_keys, far_keys = order(
        input_grad, mine, tok_rows, d_query, d_values, d_keys, parts, orders
    )
    def with_vectors(held, side, first):
        extra = lax.dynamic_index_in_dim(small_in, side[0], 1, keepdims=False)
        extra = extra[first : first + held.shape[0]]
        return lax.dynamic_update_slice(held, extra, (0, 2 * own, 0))

    near = with_vectors(near, mine, 0)
    far = [with_vectors(member, other, at * parts // 2) for at, member in enumerate(far)]
    input_sum = Reduce(order, shards + chip, near, *far)
    keys_sum = Reduce(order, [("fsdp", bit) for bit in turned] + chip, near_keys, far_keys)
    up_sum.step()
    down_sum.step()
    tokens_grad.step()
    input_sum.step()
    keys_sum.step()
    up_sum.step()
    down_sum.step()
    layer_out.step()
    input_sum.step()
    keys_sum.step()
    tokens_grad = tokens_grad.last()
    late = layer_out
    chains = {"up": up_sum, "down": down_sum, "input": input_sum, "keys": keys_sum}
    done = {}
    while chains:
        for name, chain in list(chains.items()):
            if chain.route:
                chain.step()
            else:
                done[name] = chain.last()
                del chains[name]
        if late is not None:
            layer_out, late = late.last(), None
    layer_out, tokens_grad = [member.reshape(tokens.shape) for member in (layer_out, tokens_grad)]
    up_done, down_done, input_done, keys_done = [
        done[name] for name in ("up", "down", "input", "keys")
    ]

    def across(value):
        lower, upper = both(jnp.stack(both(value, "ctx", 1)), "ctx", 0)
        return [lower[0], upper[0], lower[1], upper[1]]

    def joined(members):
        return jnp.concatenate(members, axis=1).astype(WIDE)

    lower, upper = both(down_done, "ctx", 0)
    down_result = jnp.concatenate([lower, upper], axis=0).astype(WIDE).T

    blocks = across(up_done)
    span = up_weight.shape[1] // ranks
    up_result = joined([member[:, :span] for member in blocks])
    output_result = joined([member[:, span:] for member in blocks])

    sides, keys_sides = both(input_done, "ctx", 0), both(keys_done, "ctx", 0)
    query_result, value_result = [[side[at * own : (at + 1) * own] for side in sides] for at in range(2)]
    input_result = joined([*query_result, *keys_sides, *value_result])
    flat = jnp.concatenate([side[2 * own :].reshape(-1) for side in sides]).astype(WIDE)
    eight = [flat[at * own : (at + 1) * own] for at in range(8)]
    up_bias_grad = flat[8 * own : 8 * own + deep]

    return (
        layer_out,
        tokens_grad,
        input_result,
        output_result,
        up_result,
        down_result,
        *eight[:5],
        up_bias_grad,
        *eight[5:],
    )


def solution(mesh):
    rows = P("fsdp", "ctx", None)
    matrix = P("fsdp", None)
    vector = P("fsdp")
    return jax.shard_map(
        local,
        mesh=mesh,
        in_specs=(rows,) * 2 + (matrix,) * 4 + (vector,) * 9,
        out_specs=(rows,) * 2 + (matrix,) * 4 + (vector,) * 9,
        check_vma=False,
    )
```
